128 devices in a mesh: row: 8 (over x, y_hi), col: 16 (over y_lo, z, core).
Axes of the slice: x: 4, y: 4 (y_hi: 2, y_lo: 2; y = y_hi * 2 + y_lo), z: 4, core: 2. Of those that a mesh axis runs over, the one named last changes fastest.
Arguments:
- queries: float32 [2, 384, 20480], P(None, 'col', 'row'), may hold values from -6 to 6
- precond: float32 [20480, 20480], P('row', 'col'), may hold values from -0.0390625 to 0.0390625
- column_gain: float32 [20480], P('col'), may hold values from 0.5 to 2
- store: bfloat16 [24576, 20480], P('row', 'col'), may hold values from -0.0390625 to 0.0390625
Outputs:
- scores: float32 [2, 384, 24576], P(None, 'col', 'row')
The draws below stay inside these ranges and needn't reach their ends.
All inputs are finite; a program needn't handle non-finite values.
Results may differ from the reference program's by a relative error of at most 0.0029.
Values sent between devices are 32-bit elements; how exact they have to be, the bound alone decides.
A program may use at most 128 MiB of HBM per device.

```python
import math
import jax
import jax.numpy as jnp
from jax import lax

G = 20480
BATCHES = 2
QB = 384
DOCS = 24576


def block_levels(own_key, extent, cuts, least, top_value):
    level, own = 1.0, jax.random.fold_in(own_key, 6)
    for axis_at, parts in cuts:
        steps = jnp.exp(jax.random.uniform(jax.random.fold_in(own, axis_at), (parts,), jnp.float32, least / len(cuts), top_value / len(cuts)))
        level = level * jnp.repeat(steps, extent[axis_at] // parts).reshape([-1 if axis == axis_at else 1 for axis in range(len(extent))])
    return level


def gaussian(own_key, dims, width, reach, pieces=(), held_as=jnp.bfloat16):
    array = width * jax.random.normal(own_key, dims, jnp.float32)
    if pieces:
        array = array * block_levels(own_key, dims, pieces, -0.22, 0.18)
    return jnp.clip(array, -reach, reach).astype(held_as)


def setup_inputs(seed: int = 0) -> dict:
    seeds = jax.random.split(jax.random.key(seed), 5)
    return {
        "queries": gaussian(seeds[0], (BATCHES, QB, G), 1.0, 6.0, ((1, 16), (2, 8)), jnp.float32),
        "precond": gaussian(seeds[1], (G, G), G ** -0.5, 0.0390625, ((0, 8), (1, 16)), jnp.float32),
        "column_gain": jnp.clip(jnp.exp(math.log(2.0) - 1.3862944 * jax.random.uniform(seeds[2], (G,), jnp.float32) ** block_levels(seeds[2], (G,), ((0, 16),), -0.2, 0.2)), 0.5, 2.0),
        "store": gaussian(seeds[3], (DOCS, G), G ** -0.5, 0.0390625, ((0, 8), (1, 16))),
    }


def reference(queries, precond, column_gain, store):
    results = []
    for batch_index in range(BATCHES):
        conditioned = jnp.dot(queries[batch_index], precond, precision=lax.Precision.HIGHEST, preferred_element_type=jnp.float32)
        lowered = (conditioned * column_gain[None, :]).astype(jnp.bfloat16)
        results.append(jnp.dot(lowered, store.T, preferred_element_type=jnp.float32))
    return jnp.stack(results)
```

```python
import functools

import jax
import jax.numpy as jnp
from jax import lax
from jax.experimental import pallas as pl
from jax.experimental.pallas import tpu as pltpu
from jax.sharding import PartitionSpec as P

MESH = pl.DeviceIdType.MESH
Q = 8
PT = 128
F32, BF16 = jnp.float32, jnp.bfloat16


def kernel(
    n, qin, gain, precond, store, out,
    qg, qs, phi, plo, stage, p1, rx, ty, ry, low, lowb, sv, p2, rc, rz, tc, rl,
    pt_sem, st_sem, a_s, az_r, ay_r, ac_r, b_s, bx_r, by_r, bh_r, bg_r, c_s, cc_r, cz_r, cy_r,
):
    q = Q
    K, N1, N2 = phi.shape[0], phi.shape[1], sv.shape[0]
    row, col = lax.axis_index("row"), lax.axis_index("col")
    x, yh = row // 2, lax.rem(row, 2)
    yl, z, c = col // 8, lax.rem(col // 2, 4), lax.rem(col, 2)

    def dev(x=x, yh=yh, yl=yl, z=z, c=c):
        return (x * 2 + yh, yl * 8 + z * 2 + c)

    def mod4(v):
        return lax.rem(v + 4, 4)

    xn = [dev(x=mod4(x + d)) for d in (1, 2, 3)]
    zn = [dev(z=mod4(z + d)) for d in (1, 2, 3)]
    yln, yhn, cn = dev(yl=1 - yl), dev(yh=1 - yh), dev(c=1 - c)

    def rows(start, size):
        return pl.ds(pl.multiple_of(start, q), size)

    def slot(c, yl, z):
        return ((c * 2 + yl) * 4 + z) * q

    mine = rows(slot(c, yl, z), q)

    def rcopy(src, dst, ssem, rsem, device):
        return pltpu.make_async_remote_copy(
            src_ref=src, dst_ref=dst, send_sem=ssem, recv_sem=rsem, device_id=device, device_id_type=MESH
        )

    def a_z(k, d):
        return rcopy(qin.at[rows(k * q, q)], qg.at[k, mine], a_s.at[k, d - 1], az_r.at[k, d - 1], zn[d - 1])

    def a_z_in(k, d):
        there = qg.at[k, rows(slot(c, yl, mod4(z - d)), q)]
        return rcopy(there, there, a_s.at[k, d - 1], az_r.at[k, d - 1], zn[d - 1])

    def a_y(k):
        return rcopy(qin.at[rows(k * q, q)], qg.at[k, mine], a_s.at[k, 3], ay_r.at[k], yln)

    def a_yf(k, d):
        there = qg.at[k, rows(slot(c, yl, mod4(z - d)), q)]
        return rcopy(there, there, a_s.at[k, 3 + d], ay_r.at[k], yln)

    def a_y_in(k):
        there = qg.at[k, rows(slot(c, 1 - yl, 0), 4 * q)]
        return rcopy(there, there, a_s.at[k, 3], ay_r.at[k], yln)

    def a_c(k, i):
        there = qg.at[k, rows(slot(c, yl if i == 0 else 1 - yl, 0), 4 * q)]
        return rcopy(there, there, a_s.at[k, 7 + i], ac_r.at[k], cn)

    def a_c_in(k):
        there = qg.at[k, rows(slot(1 - c, 0, 0), 8 * q)]
        return rcopy(there, there, a_s.at[k, 7], ac_r.at[k], cn)

    def b_x(k, d):
        src = p1.at[lax.rem(k, 2), rows(mod4(x + d) * 4 * q, 4 * q)]
        return rcopy(src, rx.at[k, d - 1], b_s.at[k, d - 1], bx_r.at[k, d - 1], xn[d - 1])

    def b_y(k):
        return rcopy(ty.at[k], ry.at[k], b_s.at[k, 3], by_r.at[k], yhn)

    def lrows(x, yh):
        return rows(x * 4 * q + yh * 2 * q, 2 * q)

    def b_g(k, d):
        there = low.at[k, lrows(x, yh)]
        return rcopy(there, there, b_s.at[k, 3 + d], bg_r.at[k, d - 1], xn[d - 1])

    def b_h(k):
        there = low.at[k, lrows(x, yh)]
        return rcopy(there, there, b_s.at[k, 7], bh_r.at[k], yhn)

    def b_h_in(k):
        there = low.at[k, lrows(x, 1 - yh)]
        return rcopy(there, there, b_s.at[k, 7], bh_r.at[k], yhn)

    def b_gf(k, d):
        there = low.at[k, lrows(x, 1 - yh)]
        return rcopy(there, there, b_s.at[k, 7 + d], bg_r.at[k, d - 1], xn[d - 1])

    def b_g_in(k, d):
        there = low.at[k, rows(mod4(x - d) * 4 * q, 4 * q)]
        return rcopy(there, there, b_s.at[k, 3 + d], bg_r.at[k, d - 1], xn[d - 1])

    def c_c(k):
        src = p2.at[lax.rem(k, 2), rows(slot(1 - c, 0, 0), 8 * q)]
        return rcopy(src, rc.at[k], c_s.at[k, 0], cc_r.at[k], cn)

    def c_z(k, d, l):
        src = p2.at[lax.rem(k, 2), rows(slot(c, l, mod4(z + d)), q)]
        return rcopy(src, rz.at[k, d - 1, l], c_s.at[k, 2 * d - 1 + l], cz_r.at[k, d - 1], zn[d - 1])

    def c_z_in(k, d):
        there = rz.at[k, d - 1]
        return rcopy(there, there, c_s.at[k, 2 * d - 1], cz_r.at[k, d - 1], zn[d - 1])

    def c_y(k):
        return rcopy(tc.at[k], rl.at[k], c_s.at[k, 7], cy_r.at[k], yln)

    def A1(k):
        qg[k, mine] = qin[rows(k * q, q)]
        for d in (1, 3, 2):
            a_z(k, d).start()
        a_y(k).start()

    def A2(k):
        for d in (1, 3, 2):
            a_z_in(k, d).wait_recv()
            a_yf(k, d).start()
        a_c(k, 0).start()

    def A3(k):
        a_y_in(k).wait_recv()
        a_c(k, 1).start()

    def M1(k):
        a_c_in(k).wait_recv()

        @pl.when(k >= 2)
        def _():
            for d in (1, 2, 3):
                b_x(k - 2, d).wait_send()

        def split(i, _):
            part = rows(i * 16, 16)
            v = qg[k, part]
            hi = v.astype(BF16)
            qs[part] = hi
            qs[rows(16 * q + i * 16, 16)] = (v - hi.astype(F32)).astype(BF16)
            return 0

        lax.fori_loop(0, q, split, 0)

        def tile(j, _):
            cols = pl.ds(pl.multiple_of(j * 256, 256), 256)
            both = jnp.dot(qs[...], phi[:, cols], preferred_element_type=F32)
            third = jnp.dot(qs[: 16 * q], plo[:, cols], preferred_element_type=F32)
            p1[lax.rem(k, 2), :, cols] = both[: 16 * q] + (both[16 * q :] + third)
            return 0

        lax.fori_loop(0, N1 // 256, tile, 0)
        for d in (2, 1, 3):
            b_x(k, d).start()

    def B2(k):
        for d in (1, 2, 3):
            b_x(k, d).wait_recv()
        at = x * 4 * q

        def total(h):
            own = p1[lax.rem(k, 2), rows(at + h * 2 * q, 2 * q)]
            part = rows(h * 2 * q, 2 * q)
            return (own + rx[k, 0, part]) + (rx[k, 1, part] + rx[k, 2, part])

        ty[k] = total(1 - yh)
        b_y(k).start()
        low[k, lrows(x, yh)] = total(yh)

    def B3(k):
        b_y(k).wait_recv()
        here = lrows(x, yh)
        v = (low[k, here] + ry[k]) * gain[...]
        low[k, here] = v.astype(BF16).astype(F32)
        b_h(k).start()
        for d in (2, 1, 3):
            b_g(k, d).start()

    def B5(k):
        b_h_in(k).wait_recv()
        for d in (2, 1, 3):
            b_gf(k, d).start()

    def M2(k):
        for d in (1, 2, 3):
            b_g_in(k, d).wait_recv()

        @pl.when(k >= 2)
        def _():
            c_c(k - 2).wait_send()
            for d in (1, 2, 3):
                for l in (0, 1):
                    c_z(k - 2, d, l).wait_send()

        lowb[...] = low[k].astype(BF16)

        def tile(j, _):
            cols = pl.ds(pl.multiple_of(j * 256, 256), 256)
            p2[lax.rem(k, 2), :, cols] = lax.dot_general(
                lowb[...], sv[cols, :], (((1,), (1,)), ((), ())), preferred_element_type=F32
            )
            return 0

        lax.fori_loop(0, N2 // 256, tile, 0)
        c_c(k).start()

    def C1(k):
        c_c(k).wait_recv()
        here = rows(slot(c, 0, 0), 8 * q)
        p2[lax.rem(k, 2), here] = p2[lax.rem(k, 2), here] + rc[k]
        for d in (2, 1, 3):
            for l in (0, 1):
                c_z(k, d, l).start()

    def C2(k):
        for d in (1, 2, 3):
            c_z_in(k, d).wait_recv()

        def total(l):
            own = p2[lax.rem(k, 2), rows(slot(c, l, z), q)]
            return (own + rz[k, 0, l]) + (rz[k, 1, l] + rz[k, 2, l])

        tc[k] = total(1 - yl)
        c_y(k).start()
        out[rows(k * q, q)] = total(yl)

    def C3(k):
        c_y(k).wait_recv()
        out[rows(k * q, q)] = out[rows(k * q, q)] + rl[k]

    barrier = pltpu.get_barrier_semaphore()
    for peer in xn + zn + [yln, yhn, cn]:
        pl.semaphore_signal(barrier, inc=1, device_id=peer, device_id_type=MESH)

    def p_in(i):
        return pltpu.make_async_copy(
            precond.at[pl.ds(pl.multiple_of(i * PT, PT), PT)], stage.at[lax.rem(i, 2)], pt_sem.at[lax.rem(i, 2)]
        )

    p_in(0).start()
    p_in(1).start()
    s_in = pltpu.make_async_copy(store, sv, st_sem)
    pl.semaphore_wait(barrier, 9)
    A1(0)

    def split_p(i, _):
        p_in(i).wait()
        part = pl.ds(pl.multiple_of(i * PT, PT), PT)
        v = stage[lax.rem(i, 2)]
        hi = v.astype(BF16)
        phi[part] = hi
        plo[part] = (v - hi.astype(F32)).astype(BF16)

        @pl.when(i + 2 < K // PT)
        def _():
            p_in(i + 2).start()

        return 0

    half = K // PT // 2
    lax.fori_loop(0, half, split_p, 0)
    A2(0)
    A1(1)
    lax.fori_loop(half, K // PT, split_p, 0)
    s_in.start()
    A3(0)
    s_in.wait()

    def step(s, _):
        def at(task, k):
            @pl.when((k >= 0) & (k < n))
            def _():
                task(k)

        at(M1, s)
        at(A1, s + 2)
        at(A2, s + 1)
        at(B2, s - 1)
        at(C2, s - 3)
        at(M2, s - 2)
        at(B3, s - 1)
        at(C1, s - 2)
        at(B5, s - 1)
        at(A3, s + 1)
        at(C3, s - 3)
        return 0

    lax.fori_loop(0, n + 3, step, 0)

    def drain(k, _):
        for d in (1, 2, 3):
            a_z(k, d).wait_send()
            a_yf(k, d).wait_send()
            b_g(k, d).wait_send()
            b_gf(k, d).wait_send()
        a_y(k).wait_send()
        a_c(k, 0).wait_send()
        a_c(k, 1).wait_send()
        b_y(k).wait_send()
        b_h(k).wait_send()
        c_y(k).wait_send()

        @pl.when(k >= n - 2)
        def _():
            c_c(k).wait_send()
            for d in (1, 2, 3):
                b_x(k, d).wait_send()
                for l in (0, 1):
                    c_z(k, d, l).wait_send()

        return 0

    lax.fori_loop(0, n, drain, 0)


def local(queries, precond, column_gain, store):
    b, own, K = queries.shape
    q, N1, N2 = Q, precond.shape[1], store.shape[0]
    n = b * own // q
    vm = pltpu.VMEM
    dma = pltpu.SemaphoreType.DMA
    out = pl.pallas_call(
        functools.partial(kernel, n),
        out_shape=jax.ShapeDtypeStruct((b * own, N2), F32),
        in_specs=[
            pl.BlockSpec(memory_space=pltpu.VMEM),
            pl.BlockSpec(memory_space=pltpu.VMEM),
            pl.BlockSpec(memory_space=pl.ANY),
            pl.BlockSpec(memory_space=pl.ANY),
        ],
        out_specs=pl.BlockSpec(memory_space=pltpu.VMEM),
        scratch_shapes=[
            vm((n, 16 * q, K), F32),
            vm((32 * q, K), BF16),
            vm((K, N1), BF16),
            vm((K, N1), BF16),
            vm((2, PT, N1), F32),
            vm((2, 16 * q, N1), F32),
            vm((n, 3, 4 * q, N1), F32),
            vm((n, 2 * q, N1), F32),
            vm((n, 2 * q, N1), F32),
            vm((n, 16 * q, N1), F32),
            vm((16 * q, N1), BF16),
            vm((N2, N1), BF16),
            vm((2, 16 * q, N2), F32),
            vm((n, 8 * q, N2), F32),
            vm((n, 3, 2, q, N2), F32),
            vm((n, q, N2), F32),
            vm((n, q, N2), F32),
            dma((2,)),
            dma,
            dma((n, 9)),
            dma((n, 3)),
            dma((n,)),
            dma((n,)),
            dma((n, 11)),
            dma((n, 3)),
            dma((n,)),
            dma((n,)),
            dma((n, 3)),
            dma((n, 8)),
            dma((n,)),
            dma((n, 3)),
            dma((n,)),
        ],
        compiler_params=pltpu.CompilerParams(
            collective_id=0, has_side_effects=True, vmem_limit_bytes=63 * 1024 * 1024
        ),
        cost_estimate=pl.CostEstimate(flops=2 * 16 * b * own * (3 * K * N1 + N1 * N2), bytes_accessed=24 << 20, transcendentals=0),
        name="scores",
    )(queries.reshape(b * own, K), column_gain.reshape(1, N1), precond, store)
    return out.reshape(b, own, N2)


def solution(mesh):
    return jax.shard_map(
        local,
        mesh=mesh,
        in_specs=(P(None, "col", "row"), P("row", "col"), P("col"), P("row", "col")),
        out_specs=P(None, "col", "row"),
        check_vma=False,
    )
```

```python
import functools

import jax
import jax.numpy as jnp
from jax import lax
from jax.experimental import pallas as pl
from jax.experimental.pallas import tpu as pltpu
from jax.sharding import PartitionSpec as P

MESH = pl.DeviceIdType.MESH
Q = 8
PT, NB = 128, 4
S1, S2 = 3, 3
T1, T2 = 1280, 1024
ORDER = (
    ("A1", 0), ("A1", 1), ("PR", 0), ("PR", 1), ("A2y", 0), ("A2y", 1), ("A2z", 0), ("A2c", 0), ("ST", 0),
    ("A2z", 1), ("A2c", 1), ("ST", 1), ("ST", 2), ("A3", 0), ("A1", 2), ("A3", 1), ("A1", 3), ("M1", 0),
    ("A2y", 2), ("A2y", 3), ("M1", 1), ("B1y", 0), ("A2z", 2), ("A2c", 2), ("A2z", 3), ("A2c", 3), ("B2", 0),
    ("B1y", 1), ("B2", 1), ("A3", 2), ("A3", 3), ("A1", 4), ("B3", 0), ("A1", 5), ("B3", 1), ("M1", 2),
    ("M1", 3), ("B5", 0), ("B6a", 0), ("A2y", 4), ("B5", 1), ("B6a", 1), ("A2z", 4), ("A2c", 4), ("A2y", 5),
    ("A2z", 5), ("A2c", 5), ("B1y", 2), ("B1y", 3), ("M2", 0), ("B2", 2), ("A3", 4), ("A3", 5), ("M2", 1),
    ("B2", 3), ("B3", 2), ("M1", 4), ("C1", 0), ("C1", 1), ("B5", 2), ("B3", 3), ("B6a", 2), ("M1", 5),
    ("B1y", 4), ("B6a", 3), ("C1y", 0), ("C2", 0), ("B5", 3), ("M2", 2), ("C1y", 1), ("C2", 1), ("B2", 4),
    ("B1y", 5), ("C1", 2), ("C3", 0), ("B2", 5), ("M2", 3), ("B3", 4), ("C3", 1), ("C1", 3), ("B3", 5),
    ("C1y", 2), ("C2", 2), ("B6a", 4), ("B5", 4), ("B6a", 5), ("C1y", 3), ("C2", 3), ("B5", 5), ("M2", 4),
    ("C3", 2), ("M2", 5), ("C3", 3), ("C1", 4), ("C1", 5), ("C1y", 4), ("C1y", 5), ("C2", 4), ("C3", 4),
    ("C2", 5), ("C3", 5),
)
F32, BF16 = jnp.float32, jnp.bfloat16


def kernel(
    n, qin, gain, precond, store, out,
    qg, qs, phi, plo, stage, p1, rx, rx2, ry, low, lowb, sv, sst, p2, rc, rz, rz2, rl,
    pt_sem, st_sem, a_s, az_r, azf_r, ay_r, ac_r, b_s, bx_r, by_r, bh_r, bg_r, bgf_r, c_s, cc_r, cz_r, cz2_r, cy_r,
):
    q = Q
    K, N1, N2 = phi.shape[0], phi.shape[1], sv.shape[1]
    row, col = lax.axis_index("row"), lax.axis_index("col")
    x, yh = row // 2, lax.rem(row, 2)
    yl, z, c = col // 8, lax.rem(col // 2, 4), lax.rem(col, 2)

    def dev(x=x, yh=yh, yl=yl, z=z, c=c):
        return (x * 2 + yh, yl * 8 + z * 2 + c)

    def mod4(v):
        return lax.rem(v + 4, 4)

    xn = [dev(x=mod4(x + d)) for d in (1, 2, 3)]
    zn = [dev(z=mod4(z + d)) for d in (1, 2, 3)]
    yln, yhn, cn = dev(yl=1 - yl), dev(yh=1 - yh), dev(c=1 - c)

    def rows(start, size):
        return pl.ds(pl.multiple_of(start, q), size)

    def slot(c, yl, z):
        return ((c * 2 + yl) * 4 + z) * q

    mine = rows(slot(c, yl, z), q)

    def rcopy(src, dst, ssem, rsem, device):
        return pltpu.make_async_remote_copy(
            src_ref=src, dst_ref=dst, send_sem=ssem, recv_sem=rsem, device_id=device, device_id_type=MESH
        )

    def at_slot(k, c, l, zz, count=1):
        return qg.at[k, rows(slot(c, l, zz), count * q)]

    def same(there, ssem, rsem, device):
        return rcopy(there, there, ssem, rsem, device)

    def own(k):
        return qin.at[rows(k * q, q)]

    def a_z(k, d):
        return rcopy(own(k), qg.at[k, mine], a_s.at[k, d - 1], az_r.at[k, d - 1], zn[d - 1])

    def a_z_in(k, d):
        return same(at_slot(k, c, yl, mod4(z - d)), a_s.at[k, d - 1], az_r.at[k, d - 1], zn[d - 1])

    def a_y(k):
        return rcopy(own(k), qg.at[k, mine], a_s.at[k, 3], ay_r.at[k, 0], yln)

    def a_y_in(k):
        return same(at_slot(k, c, 1 - yl, z), a_s.at[k, 3], ay_r.at[k, 0], yln)

    def a_zf(k, d):
        return same(at_slot(k, c, 1 - yl, z), a_s.at[k, 3 + d], azf_r.at[k, d - 1], zn[d - 1])

    def a_zf_in(k, d):
        return same(at_slot(k, c, 1 - yl, mod4(z - d)), a_s.at[k, 3 + d], azf_r.at[k, d - 1], zn[d - 1])

    def a_yf(k):
        return same(at_slot(k, c, yl, mod4(z + 2)), a_s.at[k, 5], ay_r.at[k, 1], yln)

    def a_yf_in(k):
        return same(at_slot(k, c, 1 - yl, mod4(z + 2)), a_s.at[k, 5], ay_r.at[k, 1], yln)

    def a_c(k, i):
        return same(at_slot(k, c, yl if i == 0 else 1 - yl, 0, 4), a_s.at[k, 7 + i], ac_r.at[k, i], cn)

    def a_c_in(k, i):
        return same(at_slot(k, 1 - c, yl if i == 0 else 1 - yl, 0, 4), a_s.at[k, 7 + i], ac_r.at[k, i], cn)

    def lrows(x, yh):
        return rows(x * 4 * q + yh * 2 * q, 2 * q)

    x2 = mod4(x + 2)
    z2 = mod4(z + 2)

    def b_y1(k):
        return rcopy(p1.at[k % S1, lrows(x2, 1 - yh)], ry.at[k, 0], b_s.at[k, 0], by_r.at[k, 0], yhn)

    def b_x(k, d):
        src = p1.at[k % S1, rows(mod4(x + d) * 4 * q, 4 * q)]
        return rcopy(src, rx.at[k, d // 2], b_s.at[k, d], bx_r.at[k, d - 1], xn[d - 1])

    def b_x2(k):
        return rcopy(ry.at[k, 0], rx2.at[k], b_s.at[k, 2], bx_r.at[k, 1], xn[1])

    def b_y(k):
        return rcopy(rx.at[k, 0, rows((1 - yh) * 2 * q, 2 * q)], ry.at[k, 1], b_s.at[k, 4], by_r.at[k, 1], yhn)

    def b_g(k, d):
        return same(low.at[k, lrows(x, yh)], b_s.at[k, 4 + d], bg_r.at[k, d - 1], xn[d - 1])

    def b_g_in(k, d):
        return same(low.at[k, lrows(mod4(x - d), yh)], b_s.at[k, 4 + d], bg_r.at[k, d - 1], xn[d - 1])

    def b_h(k):
        return same(low.at[k, lrows(x, yh)], b_s.at[k, 8], bh_r.at[k, 0], yhn)

    def b_h_in(k):
        return same(low.at[k, lrows(x, 1 - yh)], b_s.at[k, 8], bh_r.at[k, 0], yhn)

    def b_gf(k, d):
        return same(low.at[k, lrows(x, 1 - yh)], b_s.at[k, 8 + d], bgf_r.at[k, d - 1], xn[d - 1])

    def b_gf_in(k, d):
        return same(low.at[k, lrows(mod4(x - d), 1 - yh)], b_s.at[k, 8 + d], bgf_r.at[k, d - 1], xn[d - 1])

    def b_hf(k):
        return same(low.at[k, lrows(x2, yh)], b_s.at[k, 10], bh_r.at[k, 1], yhn)

    def b_hf_in(k):
        return same(low.at[k, lrows(x2, 1 - yh)], b_s.at[k, 10], bh_r.at[k, 1], yhn)

    def part(k, l, zz):
        return p2.at[k % S2, rows(slot(c, l, zz), q)]

    def c_c(k):
        return rcopy(p2.at[k % S2, rows(slot(1 - c, 0, 0), 8 * q)], rc.at[k], c_s.at[k, 0], cc_r.at[k], cn)

    def c_y1(k):
        return rcopy(part(k, 1 - yl, z2), rl.at[k, 0], c_s.at[k, 1], cy_r.at[k, 0], yln)

    def c_zd(k, d):
        return rcopy(part(k, yl, mod4(z + d)), rz.at[k, d // 2, 0], c_s.at[k, 1 + d], cz_r.at[k, d // 2, 0], zn[d - 1])

    def c_zr(k, d):
        return rcopy(part(k, 1 - yl, mod4(z + d)), rz.at[k, d // 2, 1], c_s.at[k, 4 + d], cz_r.at[k, d // 2, 1], zn[d - 1])

    def c_z2(k):
        return rcopy(rl.at[k, 0], rz2.at[k], c_s.at[k, 3], cz2_r.at[k], zn[1])

    def c_y(k):
        return rcopy(rz.at[k, 0, 1], rl.at[k, 1], c_s.at[k, 6], cy_r.at[k, 1], yln)

    def A1(k):
        qg[k, mine] = qin[rows(k * q, q)]
        a_y(k).start()
        for d in (2, 1, 3):
            a_z(k, d).start()

    def A2y(k):
        a_y_in(k).wait_recv()
        for d in (1, 3):
            a_zf(k, d).start()

    def A2z(k):
        a_z_in(k, 2).wait_recv()
        a_yf(k).start()

    def A2c(k):
        for d in (1, 3):
            a_z_in(k, d).wait_recv()
        a_c(k, 0).start()

    def A3(k):
        a_yf_in(k).wait_recv()
        for d in (1, 3):
            a_zf_in(k, d).wait_recv()
        a_c(k, 1).start()

    def M1(k):
        a_c_in(k, 0).wait_recv()
        a_c_in(k, 1).wait_recv()
        if k >= S1:
            b_y1(k - S1).wait_send()
            for d in (1, 3):
                b_x(k - S1, d).wait_send()

        def split(i, _):
            part = rows(i * 16, 16)
            v = qg[k, part]
            hi = v.astype(BF16)
            qs[part] = hi
            qs[rows(16 * q + i * 16, 16)] = (v - hi.astype(F32)).astype(BF16)
            return 0

        lax.fori_loop(0, q, split, 0)
        for j in range(0, N1, T1):
            cols = pl.ds(j, T1)
            both = jnp.dot(qs[...], phi[:, cols], preferred_element_type=F32)
            third = jnp.dot(qs[: 16 * q], plo[:, cols], preferred_element_type=F32)
            p1[k % S1, :, cols] = both[: 16 * q] + (both[16 * q :] + third)
        b_y1(k).start()
        for d in (1, 3):
            b_x(k, d).start()

    def B1y(k):
        b_y1(k).wait_recv()
        ry[k, 0] = ry[k, 0] + p1[k % S1, lrows(x2, yh)]
        b_x2(k).start()

    def B2(k):
        for d in (1, 3):
            b_x(k, d).wait_recv()

        def total(h):
            there = rows(h * 2 * q, 2 * q)
            return p1[k % S1, lrows(x, h)] + (rx[k, 0, there] + rx[k, 1, there])

        rx[k, 0, rows((1 - yh) * 2 * q, 2 * q)] = total(1 - yh)
        b_y(k).start()
        low[k, lrows(x, yh)] = total(yh)

    def B3(k):
        b_y(k).wait_recv()
        b_x2(k).wait_recv()
        here = lrows(x, yh)
        v = ((low[k, here] + ry[k, 1]) + rx2[k]) * gain[...]
        low[k, here] = v.astype(BF16).astype(F32)
        b_h(k).start()
        for d in (2, 1, 3):
            b_g(k, d).start()

    def B5(k):
        b_h_in(k).wait_recv()
        for d in (1, 3):
            b_gf(k, d).start()

    def B6a(k):
        b_g_in(k, 2).wait_recv()
        b_hf(k).start()

    def M2(k):
        for d in (1, 3):
            b_g_in(k, d).wait_recv()
            b_gf_in(k, d).wait_recv()
        b_hf_in(k).wait_recv()
        if k >= S2:
            c_c(k - S2).wait_send()
            c_y1(k - S2).wait_send()
            for d in (1, 3):
                c_zd(k - S2, d).wait_send()
                c_zr(k - S2, d).wait_send()
        lowb[...] = low[k].astype(BF16)

        def tile(j, _):
            cols = pl.ds(pl.multiple_of(j * T2, T2), T2)
            p2[k % S2, :, cols] = jnp.dot(lowb[...], sv[:, cols], preferred_element_type=F32)
            return 0

        lax.fori_loop(0, N2 // T2, tile, 0)
        c_c(k).start()

    def C1(k):
        c_c(k).wait_recv()
        here = rows(slot(c, 0, 0), 8 * q)
        p2[k % S2, here] = p2[k % S2, here] + rc[k]
        c_y1(k).start()
        for d in (1, 3):
            c_zr(k, d).start()
        for d in (1, 3):
            c_zd(k, d).start()

    def C1y(k):
        c_y1(k).wait_recv()
        rl[k, 0] = rl[k, 0] + part(k, yl, z2)[...]
        c_z2(k).start()

    def C2(k):
        for d in (1, 3):
            c_zr(k, d).wait_recv()
        rz[k, 0, 1] = part(k, 1 - yl, z)[...] + (rz[k, 0, 1] + rz[k, 1, 1])
        c_y(k).start()

    def C3(k):
        for d in (1, 3):
            c_zd(k, d).wait_recv()
        c_y(k).wait_recv()
        c_z2(k).wait_recv()
        out[rows(k * q, q)] = (part(k, yl, z)[...] + (rz[k, 0, 0] + rz[k, 1, 0])) + (rl[k, 1] + rz2[k])

    barrier = pltpu.get_barrier_semaphore()
    for peer in xn + zn + [yln, yhn, cn]:
        pl.semaphore_signal(barrier, inc=1, device_id=peer, device_id_type=MESH)

    def p_in(i):
        there = pl.ds(pl.multiple_of(i * PT, PT), PT)
        return pltpu.make_async_copy(precond.at[there], stage.at[lax.rem(i, NB)], pt_sem.at[lax.rem(i, NB)])

    def s_in(i):
        there = pl.ds(pl.multiple_of(i * 256, 256), 256)
        return pltpu.make_async_copy(store.at[there], sst.at[lax.rem(i, 2)], st_sem.at[lax.rem(i, 2)])

    for i in range(NB):
        p_in(i).start()
    s_in(0).start()
    s_in(1).start()

    def split_p(i, _):
        p_in(i).wait()
        part = pl.ds(pl.multiple_of(i * PT, PT), PT)
        v = stage[lax.rem(i, NB)]
        hi = v.astype(BF16)
        phi[part] = hi
        plo[part] = (v - hi.astype(F32)).astype(BF16)

        @pl.when(i + NB < K // PT)
        def _():
            p_in(i + NB).start()

        return 0

    def turn(i, _):
        s_in(i).wait()
        sv[:, pl.ds(pl.multiple_of(i * 256, 256), 256)] = sst[lax.rem(i, 2)].T

        @pl.when(i + 2 < N2 // 256)
        def _():
            s_in(i + 2).start()

        return 0

    def PR(i):
        lax.fori_loop(i * (K // PT) // 2, (i + 1) * (K // PT) // 2, split_p, 0)

    def ST(i):
        lax.fori_loop(i * (N2 // 256) // 3, (i + 1) * (N2 // 256) // 3, turn, 0)

    pl.semaphore_wait(barrier, 9)
    steps = dict(
        PR=PR, ST=ST, A1=A1, A2y=A2y, A2z=A2z, A2c=A2c, A3=A3, M1=M1, B1y=B1y, B2=B2, B3=B3, B5=B5, B6a=B6a,
        M2=M2, C1=C1, C1y=C1y, C2=C2, C3=C3,
    )
    for name, k in ORDER:
        steps[name](k)

    for k in range(n):
        for d in (1, 2, 3):
            a_z(k, d).wait_send()
            b_g(k, d).wait_send()
        a_y(k).wait_send()
        a_yf(k).wait_send()
        for d in (1, 3):
            a_zf(k, d).wait_send()
            b_gf(k, d).wait_send()
        a_c(k, 0).wait_send()
        a_c(k, 1).wait_send()
        b_x2(k).wait_send()
        b_y(k).wait_send()
        b_h(k).wait_send()
        b_hf(k).wait_send()
        c_z2(k).wait_send()
        c_y(k).wait_send()
        if k >= n - S1:
            b_y1(k).wait_send()
            for d in (1, 3):
                b_x(k, d).wait_send()
        if k >= n - S2:
            c_c(k).wait_send()
            c_y1(k).wait_send()
            for d in (1, 3):
                c_zd(k, d).wait_send()
                c_zr(k, d).wait_send()


def local(queries, precond, column_gain, store):
    b, own, K = queries.shape
    q, N1, N2 = Q, precond.shape[1], store.shape[0]
    n = b * own // q
    vm = pltpu.VMEM
    dma = pltpu.SemaphoreType.DMA
    out = pl.pallas_call(
        functools.partial(kernel, n),
        out_shape=jax.ShapeDtypeStruct((b * own, N2), F32),
        in_specs=[
            pl.BlockSpec(memory_space=pltpu.VMEM),
            pl.BlockSpec(memory_space=pltpu.VMEM),
            pl.BlockSpec(memory_space=pl.ANY),
            pl.BlockSpec(memory_space=pl.ANY),
        ],
        out_specs=pl.BlockSpec(memory_space=pltpu.VMEM),
        scratch_shapes=[
            vm((n, 16 * q, K), F32),
            vm((32 * q, K), BF16),
            vm((K, N1), BF16),
            vm((K, N1), BF16),
            vm((NB, PT, N1), F32),
            vm((S1, 16 * q, N1), F32),
            vm((n, 2, 4 * q, N1), F32),
            vm((n, 2 * q, N1), F32),
            vm((n, 2, 2 * q, N1), F32),
            vm((n, 16 * q, N1), F32),
            vm((16 * q, N1), BF16),
            vm((N1, N2), BF16),
            vm((2, 256, N1), BF16),
            vm((S2, 16 * q, N2), F32),
            vm((n, 8 * q, N2), F32),
            vm((n, 2, 2, q, N2), F32),
            vm((n, q, N2), F32),
            vm((n, 2, q, N2), F32),
            dma((NB,)),
            dma((2,)),
            dma((n, 9)),
            dma((n, 3)),
            dma((n, 3)),
            dma((n, 2)),
            dma((n, 2)),
            dma((n, 12)),
            dma((n, 3)),
            dma((n, 2)),
            dma((n, 2)),
            dma((n, 3)),
            dma((n, 3)),
            dma((n, 8)),
            dma((n,)),
            dma((n, 2, 2)),
            dma((n,)),
            dma((n, 2)),
        ],
        compiler_params=pltpu.CompilerParams(
            collective_id=0, has_side_effects=True, vmem_limit_bytes=63 * 1024 * 1024
        ),
        cost_estimate=pl.CostEstimate(flops=2 * 16 * b * own * (3 * K * N1 + N1 * N2), bytes_accessed=24 << 20, transcendentals=0),
        name="scores",
    )(queries.reshape(b * own, K), column_gain.reshape(1, N1), precond, store)
    return out.reshape(b, own, N2)


def solution(mesh):
    return jax.shard_map(
        local,
        mesh=mesh,
        in_specs=(P(None, "col", "row"), P("row", "col"), P("col"), P("row", "col")),
        out_specs=P(None, "col", "row"),
        check_vma=False,
    )
```

```python
import functools

import jax
import jax.numpy as jnp
from jax import lax
from jax.experimental import pallas as pl
from jax.experimental.pallas import tpu as pltpu
from jax.sharding import PartitionSpec as P

MESH = pl.DeviceIdType.MESH
Q = 8
PT, NB = 128, 4
NS = 4
S1, S2 = 3, 3
T1, T2 = 1280, 1024
ORDER = (
    ("A1", 0), ("PR", 0), ("A2y", 0), ("A1", 1), ("A2z", 0), ("PR", 1), ("A2c", 0), ("A2y", 1), ("A1", 2),
    ("A3", 0), ("A2z", 1), ("A2c", 1), ("M1", 0), ("A3", 1), ("A2y", 2), ("A1", 3), ("A2z", 2), ("M1", 1),
    ("B1y", 0), ("A2y", 3), ("A2c", 2), ("A3", 2), ("A1", 4), ("A2z", 3), ("B2", 0), ("B1y", 1), ("M1", 2),
    ("B2", 1), ("A2c", 3), ("A2y", 4), ("A3", 3), ("ST", 0), ("A2z", 4), ("B3", 0), ("M1", 3), ("ST", 1),
    ("A1", 5), ("ST", 2), ("A2c", 4), ("A3", 4), ("B1y", 2), ("B5", 0), ("B2", 2), ("B6a", 0), ("A2z", 5),
    ("B3", 1), ("A2y", 5), ("A2c", 5), ("B3", 2), ("M1", 4), ("B5", 1), ("B1y", 3), ("B6a", 1), ("A3", 5),
    ("M2", 0), ("B2", 3), ("B5", 2), ("C1", 0), ("B6a", 2), ("M1", 5), ("B3", 3), ("C1y", 0), ("C2", 0),
    ("B1y", 4), ("M2", 2), ("B2", 4), ("B5", 3), ("B1y", 5), ("C1", 2), ("B6a", 3), ("M2", 1), ("B3", 4),
    ("B2", 5), ("C1y", 2), ("C1", 1), ("M2", 3), ("B6a", 4), ("B5", 4), ("C1y", 1), ("C1", 3), ("B3", 5),
    ("C2", 1), ("M2", 4), ("B6a", 5), ("C1y", 3), ("B5", 5), ("C1", 4), ("C3", 1), ("C3", 0), ("C2", 2),
    ("M2", 5), ("C2", 3), ("C1y", 4), ("C2", 4), ("C3", 2), ("C1", 5), ("C1y", 5), ("C3", 4), ("C2", 5),
    ("C3", 3), ("C3", 5),
)
F32, BF16 = jnp.float32, jnp.bfloat16


def kernel(
    n, qin, gain, precond, store, out,
    qg, qs, phi, plo, stage, p1, rx, rx2, ry, low, lowb, sv, sst, p2, rc, rz, rz2, rl,
    pt_sem, st_sem, a_s, az_r, azf_r, ay_r, ac_r, b_s, bx_r, by_r, bh_r, bg_r, bgf_r, c_s, cc_r, cz_r, cz2_r, cy_r,
):
    q = Q
    K, N1, N2 = phi.shape[0], phi.shape[1], sv.shape[1]
    row, col = lax.axis_index("row"), lax.axis_index("col")
    x, yh = row // 2, lax.rem(row, 2)
    yl, z, c = col // 8, lax.rem(col // 2, 4), lax.rem(col, 2)

    def dev(x=x, yh=yh, yl=yl, z=z, c=c):
        return (x * 2 + yh, yl * 8 + z * 2 + c)

    def mod4(v):
        return lax.rem(v + 4, 4)

    xn = [dev(x=mod4(x + d)) for d in (1, 2, 3)]
    zn = [dev(z=mod4(z + d)) for d in (1, 2, 3)]
    yln, yhn, cn = dev(yl=1 - yl), dev(yh=1 - yh), dev(c=1 - c)

    def rows(start, size):
        return pl.ds(pl.multiple_of(start, q), size)

    def slot(c, yl, z):
        return ((c * 2 + yl) * 4 + z) * q

    mine = rows(slot(c, yl, z), q)

    def rcopy(src, dst, ssem, rsem, device):
        return pltpu.make_async_remote_copy(
            src_ref=src, dst_ref=dst, send_sem=ssem, recv_sem=rsem, device_id=device, device_id_type=MESH
        )

    def at_slot(k, c, l, zz, count=1):
        return qg.at[k, rows(slot(c, l, zz), count * q)]

    def same(there, ssem, rsem, device):
        return rcopy(there, there, ssem, rsem, device)

    def own(k):
        return qin.at[rows(k * q, q)]

    def a_z(k, d):
        return rcopy(own(k), qg.at[k, mine], a_s.at[k, d - 1], az_r.at[k, d - 1], zn[d - 1])

    def a_z_in(k, d):
        return same(at_slot(k, c, yl, mod4(z - d)), a_s.at[k, d - 1], az_r.at[k, d - 1], zn[d - 1])

    def a_y(k):
        return rcopy(own(k), qg.at[k, mine], a_s.at[k, 3], ay_r.at[k, 0], yln)

    def a_y_in(k):
        return same(at_slot(k, c, 1 - yl, z), a_s.at[k, 3], ay_r.at[k, 0], yln)

    def a_zf(k, d):
        return same(at_slot(k, c, 1 - yl, z), a_s.at[k, 3 + d], azf_r.at[k, d - 1], zn[d - 1])

    def a_zf_in(k, d):
        return same(at_slot(k, c, 1 - yl, mod4(z - d)), a_s.at[k, 3 + d], azf_r.at[k, d - 1], zn[d - 1])

    def a_yf(k):
        return same(at_slot(k, c, yl, mod4(z + 2)), a_s.at[k, 5], ay_r.at[k, 1], yln)

    def a_yf_in(k):
        return same(at_slot(k, c, 1 - yl, mod4(z + 2)), a_s.at[k, 5], ay_r.at[k, 1], yln)

    def a_c(k, i):
        return same(at_slot(k, c, yl if i == 0 else 1 - yl, 0, 4), a_s.at[k, 7 + i], ac_r.at[k, i], cn)

    def a_c_in(k, i):
        return same(at_slot(k, 1 - c, yl if i == 0 else 1 - yl, 0, 4), a_s.at[k, 7 + i], ac_r.at[k, i], cn)

    def lrows(x, yh):
        return rows(x * 4 * q + yh * 2 * q, 2 * q)

    x2 = mod4(x + 2)
    z2 = mod4(z + 2)

    def b_y1(k):
        return rcopy(p1.at[k % S1, lrows(x2, 1 - yh)], ry.at[k, 0], b_s.at[k, 0], by_r.at[k, 0], yhn)

    def b_x(k, d):
        src = p1.at[k % S1, rows(mod4(x + d) * 4 * q, 4 * q)]
        return rcopy(src, rx.at[k, d // 2], b_s.at[k, d], bx_r.at[k, d - 1], xn[d - 1])

    def b_x2(k):
        return rcopy(ry.at[k, 0], rx2.at[k], b_s.at[k, 2], bx_r.at[k, 1], xn[1])

    def b_y(k):
        return rcopy(rx.at[k, 0, rows((1 - yh) * 2 * q, 2 * q)], ry.at[k, 1], b_s.at[k, 4], by_r.at[k, 1], yhn)

    def b_g(k, d):
        return same(low.at[k, lrows(x, yh)], b_s.at[k, 4 + d], bg_r.at[k, d - 1], xn[d - 1])

    def b_g_in(k, d):
        return same(low.at[k, lrows(mod4(x - d), yh)], b_s.at[k, 4 + d], bg_r.at[k, d - 1], xn[d - 1])

    def b_h(k):
        return same(low.at[k, lrows(x, yh)], b_s.at[k, 8], bh_r.at[k, 0], yhn)

    def b_h_in(k):
        return same(low.at[k, lrows(x, 1 - yh)], b_s.at[k, 8], bh_r.at[k, 0], yhn)

    def b_gf(k, d):
        return same(low.at[k, lrows(x, 1 - yh)], b_s.at[k, 8 + d], bgf_r.at[k, d - 1], xn[d - 1])

    def b_gf_in(k, d):
        return same(low.at[k, lrows(mod4(x - d), 1 - yh)], b_s.at[k, 8 + d], bgf_r.at[k, d - 1], xn[d - 1])

    def b_hf(k):
        return same(low.at[k, lrows(x2, yh)], b_s.at[k, 10], bh_r.at[k, 1], yhn)

    def b_hf_in(k):
        return same(low.at[k, lrows(x2, 1 - yh)], b_s.at[k, 10], bh_r.at[k, 1], yhn)

    def part(k, l, zz):
        return p2.at[k % S2, rows(slot(c, l, zz), q)]

    def c_c(k):
        return rcopy(p2.at[k % S2, rows(slot(1 - c, 0, 0), 8 * q)], rc.at[k], c_s.at[k, 0], cc_r.at[k], cn)

    def c_y1(k):
        return rcopy(part(k, 1 - yl, z2), rl.at[k, 0], c_s.at[k, 1], cy_r.at[k, 0], yln)

    def c_zd(k, d):
        return rcopy(part(k, yl, mod4(z + d)), rz.at[k, d // 2, 0], c_s.at[k, 1 + d], cz_r.at[k, d // 2, 0], zn[d - 1])

    def c_zr(k, d):
        return rcopy(part(k, 1 - yl, mod4(z + d)), rz.at[k, d // 2, 1], c_s.at[k, 4 + d], cz_r.at[k, d // 2, 1], zn[d - 1])

    def c_z2(k):
        return rcopy(rl.at[k, 0], rz2.at[k], c_s.at[k, 3], cz2_r.at[k], zn[1])

    def c_y(k):
        return rcopy(rz.at[k, 0, 1], rl.at[k, 1], c_s.at[k, 6], cy_r.at[k, 1], yln)

    def A1(k):
        qg[k, mine] = qin[rows(k * q, q)]
        a_y(k).start()
        for d in (2, 1, 3):
            a_z(k, d).start()

    def A2y(k):
        a_y_in(k).wait_recv()
        for d in (1, 3):
            a_zf(k, d).start()

    def A2z(k):
        a_z_in(k, 2).wait_recv()
        a_yf(k).start()

    def A2c(k):
        for d in (1, 3):
            a_z_in(k, d).wait_recv()
        a_c(k, 0).start()

    def A3(k):
        a_yf_in(k).wait_recv()
        for d in (1, 3):
            a_zf_in(k, d).wait_recv()
        a_c(k, 1).start()

    def M1(k):
        a_c_in(k, 0).wait_recv()
        a_c_in(k, 1).wait_recv()
        if k >= S1:
            b_y1(k - S1).wait_send()
            for d in (1, 3):
                b_x(k - S1, d).wait_send()

        def split(i, _):
            part = rows(i * 16, 16)
            v = qg[k, part]
            hi = v.astype(BF16)
            qs[part] = hi
            qs[rows(16 * q + i * 16, 16)] = (v - hi.astype(F32)).astype(BF16)
            return 0

        lax.fori_loop(0, q, split, 0)
        for j in range(0, N1, T1):
            cols = pl.ds(j, T1)
            both = jnp.dot(qs[...], phi[:, cols], preferred_element_type=F32)
            third = jnp.dot(qs[: 16 * q], plo[:, cols], preferred_element_type=F32)
            p1[k % S1, :, cols] = both[: 16 * q] + (both[16 * q :] + third)
        b_y1(k).start()
        for d in (1, 3):
            b_x(k, d).start()

    def B1y(k):
        b_y1(k).wait_recv()
        ry[k, 0] = ry[k, 0] + p1[k % S1, lrows(x2, yh)]
        b_x2(k).start()

    def B2(k):
        for d in (1, 3):
            b_x(k, d).wait_recv()

        def total(h):
            there = rows(h * 2 * q, 2 * q)
            return p1[k % S1, lrows(x, h)] + (rx[k, 0, there] + rx[k, 1, there])

        rx[k, 0, rows((1 - yh) * 2 * q, 2 * q)] = total(1 - yh)
        b_y(k).start()
        low[k, lrows(x, yh)] = total(yh)

    def B3(k):
        b_y(k).wait_recv()
        b_x2(k).wait_recv()
        here = lrows(x, yh)
        v = ((low[k, here] + ry[k, 1]) + rx2[k]) * gain[...].reshape(1, -1)
        low[k, here] = v.astype(BF16).astype(F32)
        b_h(k).start()
        for d in (2, 1, 3):
            b_g(k, d).start()

    def B5(k):
        b_h_in(k).wait_recv()
        for d in (1, 3):
            b_gf(k, d).start()

    def B6a(k):
        b_g_in(k, 2).wait_recv()
        b_hf(k).start()

    def M2(k):
        for d in (1, 3):
            b_g_in(k, d).wait_recv()
            b_gf_in(k, d).wait_recv()
        b_hf_in(k).wait_recv()
        if k >= S2:
            c_c(k - S2).wait_send()
            c_y1(k - S2).wait_send()
            for d in (1, 3):
                c_zd(k - S2, d).wait_send()
                c_zr(k - S2, d).wait_send()
        lowb[...] = low[k].astype(BF16)

        def tile(j, _):
            cols = pl.ds(pl.multiple_of(j * T2, T2), T2)
            p2[k % S2, :, cols] = jnp.dot(lowb[...], sv[:, cols], preferred_element_type=F32)
            return 0

        lax.fori_loop(0, N2 // T2, tile, 0)
        c_c(k).start()

    def C1(k):
        c_c(k).wait_recv()
        here = rows(slot(c, 0, 0), 8 * q)
        p2[k % S2, here] = p2[k % S2, here] + rc[k]
        c_y1(k).start()
        for d in (1, 3):
            c_zr(k, d).start()
        for d in (1, 3):
            c_zd(k, d).start()

    def C1y(k):
        c_y1(k).wait_recv()
        rl[k, 0] = rl[k, 0] + part(k, yl, z2)[...]
        c_z2(k).start()

    def C2(k):
        for d in (1, 3):
            c_zr(k, d).wait_recv()
        rz[k, 0, 1] = part(k, 1 - yl, z)[...] + (rz[k, 0, 1] + rz[k, 1, 1])
        c_y(k).start()
        out[rows(k * q, q)] = part(k, yl, z)[...]

    def C3(k):
        for d in (1, 3):
            c_zd(k, d).wait_recv()
        c_y(k).wait_recv()
        c_z2(k).wait_recv()
        here = rows(k * q, q)
        out[here] = (out[here] + (rz[k, 0, 0] + rz[k, 1, 0])) + (rl[k, 1] + rz2[k])

    barrier = pltpu.get_barrier_semaphore()
    for peer in xn + zn + [yln, yhn, cn]:
        pl.semaphore_signal(barrier, inc=1, device_id=peer, device_id_type=MESH)

    def p_in(i):
        there = pl.ds(pl.multiple_of(i * PT, PT), PT)
        return pltpu.make_async_copy(precond.at[there], stage.at[lax.rem(i, NB)], pt_sem.at[lax.rem(i, NB)])

    def s_in(i):
        there = pl.ds(pl.multiple_of(i * 256, 256), 256)
        return pltpu.make_async_copy(store.at[there], sst.at[lax.rem(i, NS)], st_sem.at[lax.rem(i, NS)])

    for i in range(NB):
        p_in(i).start()
    for i in range(NS):
        s_in(i).start()

    def split_p(i, _):
        p_in(i).wait()
        part = pl.ds(pl.multiple_of(i * PT, PT), PT)
        v = stage[lax.rem(i, NB)]
        hi = v.astype(BF16)
        phi[part] = hi
        plo[part] = (v - hi.astype(F32)).astype(BF16)

        @pl.when(i + NB < K // PT)
        def _():
            p_in(i + NB).start()

        return 0

    def turn(i, _):
        s_in(i).wait()
        sv[:, pl.ds(pl.multiple_of(i * 256, 256), 256)] = sst[lax.rem(i, NS)].T

        @pl.when(i + NS < N2 // 256)
        def _():
            s_in(i + NS).start()

        return 0

    def PR(i):
        lax.fori_loop(i * (K // PT) // 2, (i + 1) * (K // PT) // 2, split_p, 0)

    def ST(i):
        lax.fori_loop(i * (N2 // 256) // 3, (i + 1) * (N2 // 256) // 3, turn, 0)

    pl.semaphore_wait(barrier, 9)
    steps = dict(
        PR=PR, ST=ST, A1=A1, A2y=A2y, A2z=A2z, A2c=A2c, A3=A3, M1=M1, B1y=B1y, B2=B2, B3=B3, B5=B5, B6a=B6a,
        M2=M2, C1=C1, C1y=C1y, C2=C2, C3=C3,
    )
    for name, k in ORDER:
        steps[name](k)

    for k in range(n):
        for d in (1, 2, 3):
            a_z(k, d).wait_send()
            b_g(k, d).wait_send()
        a_y(k).wait_send()
        a_yf(k).wait_send()
        for d in (1, 3):
            a_zf(k, d).wait_send()
            b_gf(k, d).wait_send()
        a_c(k, 0).wait_send()
        a_c(k, 1).wait_send()
        b_x2(k).wait_send()
        b_y(k).wait_send()
        b_h(k).wait_send()
        b_hf(k).wait_send()
        c_z2(k).wait_send()
        c_y(k).wait_send()
        if k >= n - S1:
            b_y1(k).wait_send()
            for d in (1, 3):
                b_x(k, d).wait_send()
        if k >= n - S2:
            c_c(k).wait_send()
            c_y1(k).wait_send()
            for d in (1, 3):
                c_zd(k, d).wait_send()
                c_zr(k, d).wait_send()


def local(queries, precond, column_gain, store):
    b, own, K = queries.shape
    q, N1, N2 = Q, precond.shape[1], store.shape[0]
    n = b * own // q
    vm = pltpu.VMEM
    dma = pltpu.SemaphoreType.DMA
    out = pl.pallas_call(
        functools.partial(kernel, n),
        out_shape=jax.ShapeDtypeStruct((b * own, N2), F32),
        in_specs=[
            pl.BlockSpec(memory_space=pltpu.VMEM),
            pl.BlockSpec(memory_space=pltpu.VMEM),
            pl.BlockSpec(memory_space=pl.ANY),
            pl.BlockSpec(memory_space=pl.ANY),
        ],
        out_specs=pl.BlockSpec(memory_space=pltpu.VMEM),
        scratch_shapes=[
            vm((n, 16 * q, K), F32),
            vm((32 * q, K), BF16),
            vm((K, N1), BF16),
            vm((K, N1), BF16),
            vm((NB, PT, N1), F32),
            vm((S1, 16 * q, N1), F32),
            vm((n, 2, 4 * q, N1), F32),
            vm((n, 2 * q, N1), F32),
            vm((n, 2, 2 * q, N1), F32),
            vm((n, 16 * q, N1), F32),
            vm((16 * q, N1), BF16),
            vm((N1, N2), BF16),
            vm((NS, 256, N1), BF16),
            vm((S2, 16 * q, N2), F32),
            vm((n, 8 * q, N2), F32),
            vm((n, 2, 2, q, N2), F32),
            vm((n, q, N2), F32),
            vm((n, 2, q, N2), F32),
            dma((NB,)),
            dma((NS,)),
            dma((n, 9)),
            dma((n, 3)),
            dma((n, 3)),
            dma((n, 2)),
            dma((n, 2)),
            dma((n, 12)),
            dma((n, 3)),
            dma((n, 2)),
            dma((n, 2)),
            dma((n, 3)),
            dma((n, 3)),
            dma((n, 8)),
            dma((n,)),
            dma((n, 2, 2)),
            dma((n,)),
            dma((n, 2)),
        ],
        compiler_params=pltpu.CompilerParams(
            collective_id=0, has_side_effects=True, vmem_limit_bytes=63 * 1024 * 1024
        ),
        cost_estimate=pl.CostEstimate(flops=2 * 16 * b * own * (3 * K * N1 + N1 * N2), bytes_accessed=24 << 20, transcendentals=0),
        name="scores",
    )(queries.reshape(b * own, K), column_gain, precond, store)
    return out.reshape(b, own, N2)


def solution(mesh):
    return jax.shard_map(
        local,
        mesh=mesh,
        in_specs=(P(None, "col", "row"), P("row", "col"), P("col"), P("row", "col")),
        out_specs=P(None, "col", "row"),
        check_vma=False,
    )
```

```python
import functools

import jax
import jax.numpy as jnp
from jax import lax
from jax.experimental import pallas as pl
from jax.experimental.pallas import tpu as pltpu
from jax.sharding import PartitionSpec as P

MESH = pl.DeviceIdType.MESH
Q = 8
PT, NB = 128, 4
NS = 4
S1, S2 = 3, 3
CUT = 768
BS, CS = 2, 2
ORDER = (
    ("A1", 0), ("PR", 0), ("A2y", 0), ("A1", 1), ("A2z", 0), ("PR", 1), ("A2y", 1), ("A2c", 0), ("A1", 2),
    ("A3", 0), ("A2z", 1), ("A2c", 1), ("M1", 0), ("A2y", 2), ("A1", 3), ("A3", 1), ("M1", 1), ("A2z", 2),
    ("M1", 2), ("A2c", 2), ("M1", 3), ("B1y", 1), ("B2", 1), ("A3", 2), ("B1y", 0), ("A2z", 3), ("A1", 4),
    ("B2", 0), ("A2y", 3), ("B1y", 2), ("M1", 4), ("M1", 5), ("B3", 0), ("B2", 2), ("ST", 0), ("A2z", 4),
    ("B1y", 3), ("A2c", 3), ("A1", 5), ("B2", 3), ("A3", 3), ("B1y", 4), ("B1y", 5), ("B3", 1), ("M1", 6),
    ("A2y", 4), ("M1", 7), ("B3", 2), ("B5", 1), ("B2", 4), ("B3", 3), ("B2", 5), ("A2z", 5), ("B6a", 0),
    ("B6a", 1), ("B5", 0), ("A2c", 4), ("A2y", 5), ("A3", 4), ("B1y", 6), ("ST", 1), ("A2c", 5), ("ST", 2),
    ("M1", 8), ("B2", 6), ("B1y", 7), ("B6a", 2), ("M1", 9), ("B5", 3), ("B5", 2), ("A3", 5), ("B6a", 3),
    ("B2", 7), ("B3", 4), ("M2", 0), ("M2", 1), ("B3", 6), ("C1", 0), ("C1", 1), ("B3", 5), ("M1", 10),
    ("B6a", 4), ("C1y", 0), ("B5", 4), ("B1y", 8), ("B3", 7), ("B1y", 9), ("B2", 8), ("M2", 2), ("C1y", 1),
    ("B6a", 6), ("B5", 5), ("B2", 9), ("C1", 2), ("B6a", 5), ("M2", 3), ("C2", 1), ("M1", 11), ("B5", 7),
    ("C2", 0), ("C1y", 2), ("C1", 3), ("B3", 8), ("M2", 4), ("B6a", 7), ("B5", 6), ("M2", 5), ("B1y", 10),
    ("B2", 10), ("C1", 4), ("C1", 5), ("B3", 9), ("B5", 8), ("B6a", 8), ("B1y", 11), ("B2", 11), ("M2", 6),
    ("C3", 0), ("C1y", 4), ("B3", 10), ("C1y", 3), ("M2", 7), ("C1", 6), ("C1y", 5), ("B5", 9), ("B6a", 9),
    ("C1", 7), ("B3", 11), ("C1y", 6), ("C2", 3), ("C2", 2), ("B6a", 10), ("B5", 10), ("M2", 8), ("M2", 9),
    ("B6a", 11), ("C1y", 7), ("B5", 11), ("C1", 8), ("C1", 9), ("C3", 2), ("C2", 6), ("C2", 4), ("C2", 5),
    ("C3", 3), ("M2", 10), ("C3", 1), ("C2", 7), ("C1y", 8), ("M2", 11), ("C1", 10), ("C3", 6), ("C1", 11),
    ("C3", 4), ("C2", 8), ("C1y", 10), ("C1y", 9), ("C2", 10), ("C2", 9), ("C1y", 11), ("C3", 8), ("C2", 11),
    ("C3", 10), ("C3", 7), ("C3", 9), ("C3", 5), ("C3", 11),
)
F32, BF16 = jnp.float32, jnp.bfloat16


def kernel(
    n, qin, gain, precond, store, result,
    qg, qs, phi, plo, stage, p1, rx, rx2, ry, low, lowb, sv, sst, p2, rc, rz, rz2, rl, out,
    q_sem, o_sem, pt_sem, st_sem, a_s, az_r, ay_r, ac_r, b_s, bx_r, by_r, bh_r, bg_r, c_s, cc_r, cz_r, cy_r,
):
    q = Q
    K, N1, N2 = phi.shape[0], phi.shape[1], sv.shape[1]
    row, col = lax.axis_index("row"), lax.axis_index("col")
    x, yh = row // 2, lax.rem(row, 2)
    yl, z, c = col // 8, lax.rem(col // 2, 4), lax.rem(col, 2)

    def dev(x=x, yh=yh, yl=yl, z=z, c=c):
        return (x * 2 + yh, yl * 8 + z * 2 + c)

    def mod4(v):
        return lax.rem(v + 4, 4)

    xn = [dev(x=mod4(x + d)) for d in (1, 2, 3)]
    zn = [dev(z=mod4(z + d)) for d in (1, 2, 3)]
    yln, yhn, cn = dev(yl=1 - yl), dev(yh=1 - yh), dev(c=1 - c)

    def rows(start, size):
        return pl.ds(pl.multiple_of(start, q), size)

    def slot(c, yl, z):
        return ((c * 2 + yl) * 4 + z) * q

    mine = rows(slot(c, yl, z), q)

    def rcopy(src, dst, ssem, rsem, device):
        return pltpu.make_async_remote_copy(
            src_ref=src, dst_ref=dst, send_sem=ssem, recv_sem=rsem, device_id=device, device_id_type=MESH
        )

    def at_slot(k, c, l, zz, count=1):
        return qg.at[k, rows(slot(c, l, zz), count * q)]

    def same(there, ssem, rsem, device):
        return rcopy(there, there, ssem, rsem, device)

    def own(k):
        return qg.at[k, mine]

    def q_in(k):
        return pltpu.make_async_copy(qin.at[rows(k * q, q)], qg.at[k, mine], q_sem.at[k])

    def a_z(k, d):
        return rcopy(own(k), qg.at[k, mine], a_s.at[k], az_r.at[k, d % 2], zn[d - 1])

    def a_y(k):
        return rcopy(own(k), qg.at[k, mine], a_s.at[k], ay_r.at[k, 0], yln)

    def a_zf(k, d):
        return same(at_slot(k, c, 1 - yl, z), a_s.at[k], ay_r.at[k, 1], zn[d - 1])

    def a_yf(k):
        return same(at_slot(k, c, yl, mod4(z + 2)), a_s.at[k], ay_r.at[k, 1], yln)

    def a_c(k, i):
        return same(at_slot(k, c, yl if i == 0 else 1 - yl, 0, 4), a_s.at[k], ac_r.at[k], cn)

    def lrows(x, yh):
        return rows(x * 4 * q + yh * 2 * q, 2 * q)

    x2 = mod4(x + 2)
    z2 = mod4(z + 2)

    def b_y1(k):
        return rcopy(p1.at[k % (S1 * BS), lrows(x2, 1 - yh)], ry.at[k, 0], b_s.at[k, 0], by_r.at[k], yhn)

    def b_x(k, d):
        src = p1.at[k % (S1 * BS), rows(mod4(x + d) * 4 * q, 4 * q)]
        return rcopy(src, rx.at[k, d // 2], b_s.at[k, 0], bx_r.at[k, 0], xn[d - 1])

    def b_x2(k):
        return rcopy(ry.at[k, 0], rx2.at[k], b_s.at[k, 1], bx_r.at[k, 1], xn[1])

    def b_y(k):
        return rcopy(rx.at[k, 0, rows((1 - yh) * 2 * q, 2 * q)], ry.at[k, 1], b_s.at[k, 1], bx_r.at[k, 1], yhn)

    def b_g(k, d):
        return same(low.at[k, lrows(x, yh)], b_s.at[k, 2], (bh_r.at[k, 1] if d == 2 else bg_r.at[k]), xn[d - 1])

    def b_h(k):
        return same(low.at[k, lrows(x, yh)], b_s.at[k, 2], bh_r.at[k, 0], yhn)

    def b_gf(k, d):
        return same(low.at[k, lrows(x, 1 - yh)], b_s.at[k, 2], bg_r.at[k], xn[d - 1])

    def b_hf(k):
        return same(low.at[k, lrows(x2, yh)], b_s.at[k, 2], bg_r.at[k], yhn)

    def part(k, l, zz):
        return p2.at[k % (S2 * CS), rows(slot(c, l, zz), q)]

    def c_c(k):
        return rcopy(p2.at[k % (S2 * CS), rows(slot(1 - c, 0, 0), 8 * q)], rc.at[k], c_s.at[k, 0], cc_r.at[k], cn)

    def c_y1(k):
        return rcopy(part(k, 1 - yl, z2), rl.at[k, 0], c_s.at[k, 0], cy_r.at[k], yln)

    def c_zd(k, d):
        return rcopy(part(k, yl, mod4(z + d)), rz.at[k, d // 2, 0], c_s.at[k, 0], cz_r.at[k, 1], zn[d - 1])

    def c_zr(k, d):
        return rcopy(part(k, 1 - yl, mod4(z + d)), rz.at[k, d // 2, 1], c_s.at[k, 0], cz_r.at[k, 0], zn[d - 1])

    def c_z2(k):
        return rcopy(rl.at[k, 0], rz2.at[k], c_s.at[k, 1], cz_r.at[k, 1], zn[1])

    def c_y(k):
        return rcopy(rz.at[k, 0, 1], rl.at[k, 1], c_s.at[k, 1], cz_r.at[k, 1], yln)

    def came(like, sem):
        rcopy(like, like, sem, sem, cn).wait_recv()

    def went(like, sem):
        rcopy(like, like, sem, sem, cn).wait_send()

    def A1(k):
        q_in(k).wait()
        a_y(k).start()
        for d in (2, 1, 3):
            a_z(k, d).start()

    def A2y(k):
        came(qg.at[k, pl.ds(0, q)], ay_r.at[k, 0])
        for d in (1, 3):
            a_zf(k, d).start()

    def A2z(k):
        came(qg.at[k, pl.ds(0, q)], az_r.at[k, 0])
        a_yf(k).start()

    def A2c(k):
        came(qg.at[k, pl.ds(0, 2 * q)], az_r.at[k, 1])
        a_c(k, 0).start()

    def A3(k):
        came(qg.at[k, pl.ds(0, 3 * q)], ay_r.at[k, 1])
        a_c(k, 1).start()

    def M1(k):
        b, h = k // BS, k % BS
        if h == 0:
            came(qg.at[b, pl.ds(0, 8 * q)], ac_r.at[b])
            if b >= S1:
                for old in range(k - S1 * BS, k - S1 * BS + BS):
                    went(p1.at[old % (S1 * BS), pl.ds(0, 10 * q)], b_s.at[old, 0])

            def split(i, _):
                part = rows(i * 16, 16)
                v = qg[b, part]
                hi = v.astype(BF16)
                qs[part] = hi
                qs[rows(16 * q + i * 16, 16)] = (v - hi.astype(F32)).astype(BF16)
                return 0

            lax.fori_loop(0, q, split, 0)
        half = N1 // BS
        first, last = (0, CUT) if h == 0 else (CUT, N1)
        cols = pl.ds(first, last - first)
        both = jnp.dot(qs[...], phi[:, cols], preferred_element_type=F32)
        third = jnp.dot(qs[: 16 * q], plo[:, cols], preferred_element_type=F32)
        product = both[: 16 * q] + (both[16 * q :] + third)
        if h == 0:
            p1[k % (S1 * BS)] = product[:, :half]
            p1[(k + 1) % (S1 * BS), :, : CUT - half] = product[:, half:]
        else:
            p1[k % (S1 * BS), :, CUT - half :] = product
        b_y1(k).start()
        for d in (1, 3):
            b_x(k, d).start()

    def B1y(k):
        came(ry.at[k, 0], by_r.at[k])
        ry[k, 0] = ry[k, 0] + p1[k % (S1 * BS), lrows(x2, yh)]
        b_x2(k).start()

    def B2(k):
        came(rx.at[k], bx_r.at[k, 0])

        def total(h):
            there = rows(h * 2 * q, 2 * q)
            return p1[k % (S1 * BS), lrows(x, h)] + (rx[k, 0, there] + rx[k, 1, there])

        rx[k, 0, rows((1 - yh) * 2 * q, 2 * q)] = total(1 - yh)
        b_y(k).start()
        low[k, lrows(x, yh)] = total(yh)

    def gain_part(h):
        return gain[pl.ds(h * (N1 // BS), N1 // BS)].reshape(1, -1)

    def B3(k):
        came(ry.at[k], bx_r.at[k, 1])
        here = lrows(x, yh)
        v = ((low[k, here] + ry[k, 1]) + rx2[k]) * gain_part(k % BS)
        low[k, here] = v.astype(BF16).astype(F32)
        b_h(k).start()
        for d in (2, 1, 3):
            b_g(k, d).start()

    def B5(k):
        came(rx2.at[k], bh_r.at[k, 0])
        for d in (1, 3):
            b_gf(k, d).start()

    def B6a(k):
        came(rx2.at[k], bh_r.at[k, 1])
        b_hf(k).start()

    def M2(k):
        b, h = k // CS, k % CS
        if h == 0:
            for part in range(b * BS, b * BS + BS):
                came(low.at[part, pl.ds(0, 10 * q)], bg_r.at[part])
                h0 = part % BS * (N1 // BS)
                lowb[:, h0 : h0 + N1 // BS] = low[part].astype(BF16)
                went(ry.at[part], b_s.at[part, 1])
            went(qg.at[b, pl.ds(0, 15 * q)], a_s.at[b])
            if b >= S2:
                for old in range(k - S2 * CS, k - S2 * CS + CS):
                    went(p2.at[old % (S2 * CS), pl.ds(0, 13 * q)], c_s.at[old, 0])
        cols = pl.ds(h * (N2 // CS), N2 // CS)
        p2[k % (S2 * CS)] = jnp.dot(lowb[...], sv[:, cols], preferred_element_type=F32)
        c_c(k).start()

    def C1(k):
        came(rc.at[k], cc_r.at[k])
        here = rows(slot(c, 0, 0), 8 * q)
        p2[k % (S2 * CS), here] = p2[k % (S2 * CS), here] + rc[k]
        c_y1(k).start()
        for d in (1, 3):
            c_zr(k, d).start()
        for d in (1, 3):
            c_zd(k, d).start()

    def C1y(k):
        came(rz2.at[k], cy_r.at[k])
        rl[k, 0] = rl[k, 0] + part(k, yl, z2)[...]
        c_z2(k).start()

    def C2(k):
        came(rl.at[k], cz_r.at[k, 0])
        rz[k, 0, 1] = part(k, 1 - yl, z)[...] + (rz[k, 0, 1] + rz[k, 1, 1])
        c_y(k).start()
        out[rows(k // CS * q, q), pl.ds(k % CS * (N2 // CS), N2 // CS)] = part(k, yl, z)[...]

    def C3(k):
        came(rz.at[k], cz_r.at[k, 1])
        here = rows(k // CS * q, q), pl.ds(k % CS * (N2 // CS), N2 // CS)
        out[here] = (out[here] + (rz[k, 0, 0] + rz[k, 1, 0])) + (rl[k, 1] + rz2[k])

    barrier = pltpu.get_barrier_semaphore()
    for peer in xn + zn + [yln, yhn, cn]:
        pl.semaphore_signal(barrier, inc=1, device_id=peer, device_id_type=MESH)

    def p_in(i):
        there = pl.ds(pl.multiple_of(i * PT, PT), PT)
        return pltpu.make_async_copy(precond.at[there], stage.at[lax.rem(i, NB)], pt_sem.at[lax.rem(i, NB)])

    def s_in(i):
        there = pl.ds(pl.multiple_of(i * 256, 256), 256)
        return pltpu.make_async_copy(store.at[there], sst.at[lax.rem(i, NS)], st_sem.at[lax.rem(i, NS)])

    for k in range(n):
        q_in(k).start()
    for i in range(NB):
        p_in(i).start()
    for i in range(NS):
        s_in(i).start()

    def split_p(i, _):
        p_in(i).wait()
        part = pl.ds(pl.multiple_of(i * PT, PT), PT)
        v = stage[lax.rem(i, NB)]
        hi = v.astype(BF16)
        phi[part] = hi
        plo[part] = (v - hi.astype(F32)).astype(BF16)

        @pl.when(i + NB < K // PT)
        def _():
            p_in(i + NB).start()

        return 0

    def turn(i, _):
        s_in(i).wait()
        sv[:, pl.ds(pl.multiple_of(i * 256, 256), 256)] = sst[lax.rem(i, NS)].T

        @pl.when(i + NS < N2 // 256)
        def _():
            s_in(i + NS).start()

        return 0

    def PR(i):
        lax.fori_loop(i * (K // PT) // 2, (i + 1) * (K // PT) // 2, split_p, 0)

    def ST(i):
        lax.fori_loop(i * (N2 // 256) // 3, (i + 1) * (N2 // 256) // 3, turn, 0)

    pl.semaphore_wait(barrier, 9)
    steps = dict(
        PR=PR, ST=ST, A1=A1, A2y=A2y, A2z=A2z, A2c=A2c, A3=A3, M1=M1, B1y=B1y, B2=B2, B3=B3, B5=B5, B6a=B6a,
        M2=M2, C1=C1, C1y=C1y, C2=C2, C3=C3,
    )
    def o_out(k):
        return pltpu.make_async_copy(out.at[rows(k * q, q)], result.at[rows(k * q, q)], o_sem.at[k])

    left = [CS] * n
    for name, k in ORDER:
        steps[name](k)
        if name == "C3":
            left[k // CS] -= 1
            if left[k // CS] == 0:
                o_out(k // CS).start()

    for k in range(n * BS):
        went(low.at[k, pl.ds(0, 14 * q)], b_s.at[k, 2])
        if k >= (n - S1) * BS:
            went(p1.at[k % (S1 * BS), pl.ds(0, 10 * q)], b_s.at[k, 0])
    for k in range(n):
        o_out(k).wait()
    for k in range(n * CS):
        went(rl.at[k], c_s.at[k, 1])
        if k >= (n - S2) * CS:
            went(p2.at[k % (S2 * CS), pl.ds(0, 13 * q)], c_s.at[k, 0])


def local(queries, precond, column_gain, store):
    b, own, K = queries.shape
    q, N1, N2 = Q, precond.shape[1], store.shape[0]
    n = b * own // q
    nb, nc = n * BS, n * CS
    vm = pltpu.VMEM
    dma = pltpu.SemaphoreType.DMA
    out = pl.pallas_call(
        functools.partial(kernel, n),
        out_shape=jax.ShapeDtypeStruct((b * own, N2), F32),
        in_specs=[
            pl.BlockSpec(memory_space=pl.ANY),
            pl.BlockSpec(memory_space=pltpu.VMEM),
            pl.BlockSpec(memory_space=pl.ANY),
            pl.BlockSpec(memory_space=pl.ANY),
        ],
        out_specs=pl.BlockSpec(memory_space=pl.ANY),
        scratch_shapes=[
            vm((n, 16 * q, K), F32),
            vm((32 * q, K), BF16),
            vm((K, N1), BF16),
            vm((K, N1), BF16),
            vm((NB, PT, N1), F32),
            vm((S1 * BS, 16 * q, N1 // BS), F32),
            vm((nb, 2, 4 * q, N1 // BS), F32),
            vm((nb, 2 * q, N1 // BS), F32),
            vm((nb, 2, 2 * q, N1 // BS), F32),
            vm((nb, 16 * q, N1 // BS), F32),
            vm((16 * q, N1), BF16),
            vm((N1, N2), BF16),
            vm((NS, 256, N1), BF16),
            vm((S2 * CS, 16 * q, N2 // CS), F32),
            vm((nc, 8 * q, N2 // CS), F32),
            vm((nc, 2, 2, q, N2 // CS), F32),
            vm((nc, q, N2 // CS), F32),
            vm((nc, 2, q, N2 // CS), F32),
            vm((b * own, N2), F32),
            dma((n,)),
            dma((n,)),
            dma((NB,)),
            dma((NS,)),
            dma((n,)),
            dma((n, 2)),
            dma((n, 2)),
            dma((n,)),
            dma((nb, 3)),
            dma((nb, 2)),
            dma((nb,)),
            dma((nb, 2)),
            dma((nb,)),
            dma((nc, 2)),
            dma((nc,)),
            dma((nc, 2)),
            dma((nc,)),
        ],
        compiler_params=pltpu.CompilerParams(
            collective_id=0, has_side_effects=True, vmem_limit_bytes=63 * 1024 * 1024
        ),
        cost_estimate=pl.CostEstimate(flops=2 * 16 * b * own * (3 * K * N1 + N1 * N2), bytes_accessed=24 << 20, transcendentals=0),
        name="scores",
    )(queries.reshape(b * own, K), column_gain, precond, store)
    return out.reshape(b, own, N2)


def solution(mesh):
    return jax.shard_map(
        local,
        mesh=mesh,
        in_specs=(P(None, "col", "row"), P("row", "col"), P("col"), P("row", "col")),
        out_specs=P(None, "col", "row"),
        check_vma=False,
    )
```

```python
import functools

import jax
import jax.numpy as jnp
from jax import lax
from jax.experimental import pallas as pl
from jax.experimental.pallas import tpu as pltpu
from jax.sharding import PartitionSpec as P

MESH = pl.DeviceIdType.MESH
Q = 8
PT, NB = 128, 4
NS = 4
S1, S2 = 3, 3
CUT = 768
BS, CS = 2, 2
ORDER = (
    ("A1", 0), ("PR", 0), ("A2y", 0), ("A1", 1), ("A2z", 0), ("PR", 1), ("A2y", 1), ("A2c", 0), ("A1", 2),
    ("A3", 0), ("ST", 0), ("A2z", 1), ("M1", 0), ("A2y", 2), ("A2c", 1), ("A1", 3), ("A3", 1), ("M1", 1),
    ("A2z", 2), ("B1y", 0), ("B2", 0), ("M1", 2), ("A2y", 3), ("B1y", 1), ("A2c", 2), ("A1", 4), ("B2", 1),
    ("A2z", 3), ("A3", 2), ("B3", 0), ("M1", 3), ("M1", 4), ("M1", 5), ("B3", 1), ("A2y", 4), ("A1", 5),
    ("B6a", 0), ("A2c", 3), ("ST", 1), ("A2z", 4), ("A3", 3), ("B1y", 3), ("B1y", 4), ("B2", 4), ("ST", 2),
    ("B5", 1), ("B5", 0), ("B1y", 2), ("B1y", 5), ("B6a", 1), ("M1", 6), ("B2", 5), ("M1", 7), ("B2", 3),
    ("B2", 2), ("M2", 0), ("A2y", 5), ("B1y", 6), ("A2z", 5), ("A2c", 5), ("B3", 5), ("B2", 6), ("A2c", 4),
    ("A3", 4), ("B3", 4), ("M2", 1), ("B3", 2), ("C1", 0), ("B1y", 7), ("B3", 3), ("C1", 1), ("M1", 8),
    ("B2", 7), ("A3", 5), ("B6a", 4), ("B5", 5), ("B6a", 5), ("M1", 9), ("B5", 4), ("B6a", 2), ("C1y", 0),
    ("B5", 2), ("M1", 10), ("B5", 3), ("C1y", 1), ("B6a", 3), ("C2", 0), ("C2", 1), ("B3", 7), ("B3", 6),
    ("B1y", 8), ("M2", 4), ("B2", 8), ("M2", 5), ("M1", 11), ("C1", 5), ("B1y", 9), ("C3", 0), ("B2", 9),
    ("C1", 4), ("M2", 2), ("B5", 7), ("B5", 6), ("B6a", 7), ("B6a", 6), ("M2", 3), ("B1y", 10), ("B2", 10),
    ("C1y", 5), ("C1", 2), ("B3", 9), ("B3", 8), ("B1y", 11), ("B2", 11), ("M2", 6), ("C1y", 4), ("C1", 3),
    ("B3", 10), ("C1", 6), ("M2", 7), ("B5", 8), ("B6a", 9), ("B6a", 8), ("C1y", 2), ("B5", 9), ("C1", 7),
    ("B3", 11), ("C1y", 3), ("C2", 3), ("C2", 2), ("C1y", 6), ("B6a", 10), ("B5", 10), ("M2", 8), ("M2", 9),
    ("B6a", 11), ("C1y", 7), ("B5", 11), ("C1", 8), ("C2", 7), ("C2", 5), ("C2", 4), ("C1", 9), ("M2", 10),
    ("C1y", 8), ("M2", 11), ("C2", 8), ("C1", 10), ("C1", 11), ("C3", 1), ("C3", 3), ("C2", 6), ("C1y", 10),
    ("C1y", 9), ("C3", 4), ("C2", 10), ("C3", 7), ("C1y", 11), ("C2", 9), ("C2", 11), ("C3", 5), ("C3", 6),
    ("C3", 9), ("C3", 8), ("C3", 2), ("C3", 10), ("C3", 11),
)
F32, BF16 = jnp.float32, jnp.bfloat16


def kernel(
    n, qin, gain, precond, store, result,
    qg, qs, phi, plo, stage, p1, rx, rx2, ry, low, lowb, sv, sst, p2, rc, rz, rz2, rl, out,
    q_sem, o_sem, pt_sem, st_sem, a_s, az_r, ay_r, ac_r, b_s, bx_r, by_r, bh_r, bg_r, c_s, cc_r, cz_r, cy_r,
):
    q = Q
    K, N1, N2 = phi.shape[0], phi.shape[1], sv.shape[1]
    row, col = lax.axis_index("row"), lax.axis_index("col")
    x, yh = row // 2, lax.rem(row, 2)
    yl, z, c = col // 8, lax.rem(col // 2, 4), lax.rem(col, 2)

    def dev(x=x, yh=yh, yl=yl, z=z, c=c):
        return (x * 2 + yh, yl * 8 + z * 2 + c)

    def mod4(v):
        return lax.rem(v + 4, 4)

    xn = [dev(x=mod4(x + d)) for d in (1, 2, 3)]
    zn = [dev(z=mod4(z + d)) for d in (1, 2, 3)]
    yln, yhn, cn = dev(yl=1 - yl), dev(yh=1 - yh), dev(c=1 - c)

    def rows(start, size):
        return pl.ds(pl.multiple_of(start, q), size)

    def slot(c, yl, z):
        return ((c * 2 + yl) * 4 + z) * q

    mine = rows(slot(c, yl, z), q)

    def rcopy(src, dst, ssem, rsem, device):
        return pltpu.make_async_remote_copy(
            src_ref=src, dst_ref=dst, send_sem=ssem, recv_sem=rsem, device_id=device, device_id_type=MESH
        )

    def at_slot(k, c, l, zz, count=1):
        return qg.at[k, rows(slot(c, l, zz), count * q)]

    def same(there, ssem, rsem, device):
        return rcopy(there, there, ssem, rsem, device)

    def own(k):
        return qg.at[k, mine]

    def q_in(k):
        return pltpu.make_async_copy(qin.at[rows(k * q, q)], qg.at[k, mine], q_sem.at[k])

    def a_z(k, d):
        return rcopy(own(k), qg.at[k, mine], a_s.at[k], az_r.at[k, d % 2], zn[d - 1])

    def a_y(k):
        return rcopy(own(k), qg.at[k, mine], a_s.at[k], ay_r.at[k, 0], yln)

    def a_zf(k, d):
        return same(at_slot(k, c, 1 - yl, z), a_s.at[k], ay_r.at[k, 1], zn[d - 1])

    def a_yf(k):
        return same(at_slot(k, c, yl, mod4(z + 2)), a_s.at[k], ay_r.at[k, 1], yln)

    def a_c(k, i):
        return same(at_slot(k, c, yl if i == 0 else 1 - yl, 0, 4), a_s.at[k], ac_r.at[k], cn)

    def lrows(x, yh):
        return rows(x * 4 * q + yh * 2 * q, 2 * q)

    x2 = mod4(x + 2)
    z2 = mod4(z + 2)

    def b_y1(k):
        return rcopy(p1.at[k % (S1 * BS), lrows(x2, 1 - yh)], ry.at[k, 0], b_s.at[k, 0], by_r.at[k], yhn)

    def b_x(k, d):
        src = p1.at[k % (S1 * BS), rows(mod4(x + d) * 4 * q, 4 * q)]
        return rcopy(src, rx.at[k, d // 2], b_s.at[k, 0], bx_r.at[k, 0], xn[d - 1])

    def b_x2(k):
        return rcopy(ry.at[k, 0], rx2.at[k], b_s.at[k, 1], bx_r.at[k, 1], xn[1])

    def b_y(k):
        return rcopy(rx.at[k, 0, rows((1 - yh) * 2 * q, 2 * q)], ry.at[k, 1], b_s.at[k, 1], bx_r.at[k, 1], yhn)

    def b_g(k, d):
        return same(low.at[k, lrows(x, yh)], b_s.at[k, 2], (bh_r.at[k, 1] if d == 2 else bg_r.at[k]), xn[d - 1])

    def b_h(k):
        return same(low.at[k, lrows(x, yh)], b_s.at[k, 2], bh_r.at[k, 0], yhn)

    def b_gf(k, d):
        return same(low.at[k, lrows(x, 1 - yh)], b_s.at[k, 2], bg_r.at[k], xn[d - 1])

    def b_hf(k):
        return same(low.at[k, lrows(x2, yh)], b_s.at[k, 2], bg_r.at[k], yhn)

    def part(k, l, zz):
        return p2.at[k % (S2 * CS), rows(slot(c, l, zz), q)]

    def c_c(k):
        return rcopy(p2.at[k % (S2 * CS), rows(slot(1 - c, 0, 0), 8 * q)], rc.at[k], c_s.at[k, 0], cc_r.at[k], cn)

    def c_y1(k):
        return rcopy(part(k, 1 - yl, z2), rl.at[k, 0], c_s.at[k, 0], cy_r.at[k], yln)

    def c_zd(k, d):
        return rcopy(part(k, yl, mod4(z + d)), rz.at[k, d // 2, 0], c_s.at[k, 0], cz_r.at[k, 1], zn[d - 1])

    def c_zr(k, d):
        return rcopy(part(k, 1 - yl, mod4(z + d)), rz.at[k, d // 2, 1], c_s.at[k, 0], cz_r.at[k, 0], zn[d - 1])

    def c_z2(k):
        return rcopy(rl.at[k, 0], rz2.at[k], c_s.at[k, 1], cz_r.at[k, 1], zn[1])

    def c_y(k):
        return rcopy(rz.at[k, 0, 1], rl.at[k, 1], c_s.at[k, 1], cz_r.at[k, 1], yln)

    def came(like, sem):
        rcopy(like, like, sem, sem, cn).wait_recv()

    def went(like, sem):
        rcopy(like, like, sem, sem, cn).wait_send()

    def A1(k):
        q_in(k).wait()
        a_y(k).start()
        for d in (2, 1, 3):
            a_z(k, d).start()

    def A2y(k):
        came(qg.at[k, pl.ds(0, q)], ay_r.at[k, 0])
        for d in (1, 3):
            a_zf(k, d).start()

    def A2z(k):
        came(qg.at[k, pl.ds(0, q)], az_r.at[k, 0])
        a_yf(k).start()

    def A2c(k):
        came(qg.at[k, pl.ds(0, 2 * q)], az_r.at[k, 1])
        a_c(k, 0).start()

    def A3(k):
        came(qg.at[k, pl.ds(0, 3 * q)], ay_r.at[k, 1])
        a_c(k, 1).start()

    def M1(k):
        b, h = k // BS, k % BS
        if h == 0:
            came(qg.at[b, pl.ds(0, 8 * q)], ac_r.at[b])
            if b >= S1:
                for old in range(k - S1 * BS, k - S1 * BS + BS):
                    went(p1.at[old % (S1 * BS), pl.ds(0, 10 * q)], b_s.at[old, 0])

            def split(i, _):
                part = rows(i * 16, 16)
                v = qg[b, part]
                hi = v.astype(BF16)
                qs[part] = hi
                qs[rows(16 * q + i * 16, 16)] = (v - hi.astype(F32)).astype(BF16)
                return 0

            lax.fori_loop(0, q, split, 0)
        half = N1 // BS
        first, last = (0, CUT) if h == 0 else (CUT, N1)
        cols = pl.ds(first, last - first)
        both = jnp.dot(qs[...], phi[:, cols], preferred_element_type=F32)
        third = jnp.dot(qs[: 16 * q], plo[:, cols], preferred_element_type=F32)
        product = both[: 16 * q] + (both[16 * q :] + third)
        if h == 0:
            p1[k % (S1 * BS)] = product[:, :half]
            p1[(k + 1) % (S1 * BS), :, : CUT - half] = product[:, half:]
        else:
            p1[k % (S1 * BS), :, CUT - half :] = product
        b_y1(k).start()
        for d in (1, 3):
            b_x(k, d).start()

    def B1y(k):
        came(ry.at[k, 0], by_r.at[k])
        ry[k, 0] = ry[k, 0] + p1[k % (S1 * BS), lrows(x2, yh)]
        b_x2(k).start()

    def B2(k):
        came(rx.at[k], bx_r.at[k, 0])

        def total(h):
            there = rows(h * 2 * q, 2 * q)
            return p1[k % (S1 * BS), lrows(x, h)] + (rx[k, 0, there] + rx[k, 1, there])

        rx[k, 0, rows((1 - yh) * 2 * q, 2 * q)] = total(1 - yh)
        b_y(k).start()
        low[k, lrows(x, yh)] = total(yh)

    def gain_part(h):
        return gain[pl.ds(h * (N1 // BS), N1 // BS)].reshape(1, -1)

    def B3(k):
        came(ry.at[k], bx_r.at[k, 1])
        here = lrows(x, yh)
        v = ((low[k, here] + ry[k, 1]) + rx2[k]) * gain_part(k % BS)
        low[k, here] = v.astype(BF16).astype(F32)
        b_h(k).start()
        for d in (2, 1, 3):
            b_g(k, d).start()

    def B5(k):
        came(rx2.at[k], bh_r.at[k, 0])
        for d in (1, 3):
            b_gf(k, d).start()

    def B6a(k):
        came(rx2.at[k], bh_r.at[k, 1])
        b_hf(k).start()

    def M2(k):
        b, h = k // CS, k % CS
        if h == 0:
            for part in range(b * BS, b * BS + BS):
                came(low.at[part, pl.ds(0, 10 * q)], bg_r.at[part])
                h0 = part % BS * (N1 // BS)
                lowb[:, h0 : h0 + N1 // BS] = low[part].astype(BF16)
                went(ry.at[part], b_s.at[part, 1])
            went(qg.at[b, pl.ds(0, 15 * q)], a_s.at[b])
            if b >= S2:
                for old in range(k - S2 * CS, k - S2 * CS + CS):
                    went(p2.at[old % (S2 * CS), pl.ds(0, 13 * q)], c_s.at[old, 0])
        cols = pl.ds(h * (N2 // CS), N2 // CS)
        p2[k % (S2 * CS)] = jnp.dot(lowb[...], sv[:, cols], preferred_element_type=F32)
        c_c(k).start()
        if h == CS - 1:
            for part in range(b * BS, b * BS + BS):
                went(low.at[part, pl.ds(0, 14 * q)], b_s.at[part, 2])
                if b >= n - S1:
                    went(p1.at[part % (S1 * BS), pl.ds(0, 10 * q)], b_s.at[part, 0])

    def C1(k):
        came(rc.at[k], cc_r.at[k])
        here = rows(slot(c, 0, 0), 8 * q)
        p2[k % (S2 * CS), here] = p2[k % (S2 * CS), here] + rc[k]
        c_y1(k).start()
        for d in (1, 3):
            c_zr(k, d).start()
        for d in (1, 3):
            c_zd(k, d).start()

    def C1y(k):
        came(rz2.at[k], cy_r.at[k])
        rl[k, 0] = rl[k, 0] + part(k, yl, z2)[...]
        c_z2(k).start()

    def C2(k):
        came(rl.at[k], cz_r.at[k, 0])
        rz[k, 0, 1] = part(k, 1 - yl, z)[...] + (rz[k, 0, 1] + rz[k, 1, 1])
        c_y(k).start()
        out[rows(k // CS * q, q), pl.ds(k % CS * (N2 // CS), N2 // CS)] = part(k, yl, z)[...]

    def C3(k):
        came(rz.at[k], cz_r.at[k, 1])
        here = rows(k // CS * q, q), pl.ds(k % CS * (N2 // CS), N2 // CS)
        out[here] = (out[here] + (rz[k, 0, 0] + rz[k, 1, 0])) + (rl[k, 1] + rz2[k])

    barrier = pltpu.get_barrier_semaphore()
    for peer in xn + zn + [yln, yhn, cn]:
        pl.semaphore_signal(barrier, inc=1, device_id=peer, device_id_type=MESH)

    def p_in(i):
        there = pl.ds(pl.multiple_of(i * PT, PT), PT)
        return pltpu.make_async_copy(precond.at[there], stage.at[lax.rem(i, NB)], pt_sem.at[lax.rem(i, NB)])

    def s_in(i):
        there = pl.ds(pl.multiple_of(i * 256, 256), 256)
        return pltpu.make_async_copy(store.at[there], sst.at[lax.rem(i, NS)], st_sem.at[lax.rem(i, NS)])

    for k in range(n):
        q_in(k).start()
    for i in range(NB):
        p_in(i).start()
    for i in range(NS):
        s_in(i).start()

    def split_p(i, _):
        p_in(i).wait()
        part = pl.ds(pl.multiple_of(i * PT, PT), PT)
        v = stage[lax.rem(i, NB)]
        hi = v.astype(BF16)
        phi[part] = hi
        plo[part] = (v - hi.astype(F32)).astype(BF16)

        @pl.when(i + NB < K // PT)
        def _():
            p_in(i + NB).start()

        return 0

    def turn(i, _):
        s_in(i).wait()
        sv[:, pl.ds(pl.multiple_of(i * 256, 256), 256)] = sst[lax.rem(i, NS)].T

        @pl.when(i + NS < N2 // 256)
        def _():
            s_in(i + NS).start()

        return 0

    def PR(i):
        lax.fori_loop(i * (K // PT) // 2, (i + 1) * (K // PT) // 2, split_p, 0)

    def ST(i):
        lax.fori_loop(i * (N2 // 256) // 3, (i + 1) * (N2 // 256) // 3, turn, 0)

    pl.semaphore_wait(barrier, 9)
    steps = dict(
        PR=PR, ST=ST, A1=A1, A2y=A2y, A2z=A2z, A2c=A2c, A3=A3, M1=M1, B1y=B1y, B2=B2, B3=B3, B5=B5, B6a=B6a,
        M2=M2, C1=C1, C1y=C1y, C2=C2, C3=C3,
    )
    def o_out(k):
        return pltpu.make_async_copy(out.at[rows(k * q, q)], result.at[rows(k * q, q)], o_sem.at[k])

    left = [CS] * n
    for name, k in ORDER:
        steps[name](k)
        if name == "C3":
            left[k // CS] -= 1
            if left[k // CS] == 0:
                o_out(k // CS).start()

    for k in range(n):
        o_out(k).wait()
    for k in range(n * CS):
        went(rl.at[k], c_s.at[k, 1])
        if k >= (n - S2) * CS:
            went(p2.at[k % (S2 * CS), pl.ds(0, 13 * q)], c_s.at[k, 0])


def local(queries, precond, column_gain, store):
    b, own, K = queries.shape
    q, N1, N2 = Q, precond.shape[1], store.shape[0]
    n = b * own // q
    nb, nc = n * BS, n * CS
    vm = pltpu.VMEM
    dma = pltpu.SemaphoreType.DMA
    out = pl.pallas_call(
        functools.partial(kernel, n),
        out_shape=jax.ShapeDtypeStruct((b * own, N2), F32),
        in_specs=[
            pl.BlockSpec(memory_space=pl.ANY),
            pl.BlockSpec(memory_space=pltpu.VMEM),
            pl.BlockSpec(memory_space=pl.ANY),
            pl.BlockSpec(memory_space=pl.ANY),
        ],
        out_specs=pl.BlockSpec(memory_space=pl.ANY),
        scratch_shapes=[
            vm((n, 16 * q, K), F32),
            vm((32 * q, K), BF16),
            vm((K, N1), BF16),
            vm((K, N1), BF16),
            vm((NB, PT, N1), F32),
            vm((S1 * BS, 16 * q, N1 // BS), F32),
            vm((nb, 2, 4 * q, N1 // BS), F32),
            vm((nb, 2 * q, N1 // BS), F32),
            vm((nb, 2, 2 * q, N1 // BS), F32),
            vm((nb, 16 * q, N1 // BS), F32),
            vm((16 * q, N1), BF16),
            vm((N1, N2), BF16),
            vm((NS, 256, N1), BF16),
            vm((S2 * CS, 16 * q, N2 // CS), F32),
            vm((nc, 8 * q, N2 // CS), F32),
            vm((nc, 2, 2, q, N2 // CS), F32),
            vm((nc, q, N2 // CS), F32),
            vm((nc, 2, q, N2 // CS), F32),
            vm((b * own, N2), F32),
            dma((n,)),
            dma((n,)),
            dma((NB,)),
            dma((NS,)),
            dma((n,)),
            dma((n, 2)),
            dma((n, 2)),
            dma((n,)),
            dma((nb, 3)),
            dma((nb, 2)),
            dma((nb,)),
            dma((nb, 2)),
            dma((nb,)),
            dma((nc, 2)),
            dma((nc,)),
            dma((nc, 2)),
            dma((nc,)),
        ],
        compiler_params=pltpu.CompilerParams(
            collective_id=0, has_side_effects=True, vmem_limit_bytes=63 * 1024 * 1024
        ),
        cost_estimate=pl.CostEstimate(flops=2 * 16 * b * own * (3 * K * N1 + N1 * N2), bytes_accessed=24 << 20, transcendentals=0),
        name="scores",
    )(queries.reshape(b * own, K), column_gain, precond, store)
    return out.reshape(b, own, N2)


def solution(mesh):
    return jax.shard_map(
        local,
        mesh=mesh,
        in_specs=(P(None, "col", "row"), P("row", "col"), P("col"), P("row", "col")),
        out_specs=P(None, "col", "row"),
        check_vma=False,
    )
```
